128 devices in a mesh: slab: 32 (over z, x, core), col: 4 (over y).
Axes of the slice: x: 4, y: 4, z: 4, core: 2. Of those that a mesh axis runs over, the one named last changes fastest.
Arguments:
- charge: float32 [512, 256, 512], P('slab', 'col'), may hold values from -0.6 to 0.6
Outputs:
- potential: float32 [512, 256, 512], P('slab', 'col')
The draws below stay inside these ranges and needn't reach their ends.
All inputs are finite; a program needn't handle non-finite values.
Results may differ from the reference program's by a relative error of at most 0.000068.
Values sent between devices are 32-bit elements; how exact they have to be, the bound alone decides.
A program may use at most 128 MiB of HBM per device.

```python
import jax
import jax.numpy as jnp

NX = 512
NU = 2
COARSE_SWEEPS = 12
NZ = 512
NY = 256


def draw_charge(key, part):
    key = jax.random.fold_in(key, 7)
    shape = (NZ, NY, NX)
    return jnp.clip(0.08 * jax.random.normal(key, shape, jnp.float32), -0.6, 0.6)


def setup_inputs(seed: int = 0) -> dict:
    keys = jax.random.split(jax.random.key(seed), 2)
    charge = draw_charge(jax.random.fold_in(keys[1], 71), 0)
    return {"charge": charge}


kappa_sq = 0.001
omega = 0.8
four_pi = 12.566370614359172


def stencil(padded, scale):
    center = padded[1:-1, 1:-1]
    beside = padded[2:, 1:-1] + padded[:-2, 1:-1]
    beside = beside + padded[1:-1, 2:] + padded[1:-1, :-2]
    beside = beside + jnp.roll(center, 1, 2) + jnp.roll(center, -1, 2)
    return (6.0 * center - beside) * scale + kappa_sq * center


def operate(field, scale):
    return stencil(jnp.pad(field, ((1, 1), (1, 1), (0, 0)), mode="wrap"), scale)


def smooth(field, source, scale, count):
    diag = 6.0 * scale + kappa_sq
    for step in range(count):
        field = field + omega * (source - operate(field, scale)) / diag
    return field


def restrict(field):
    zsz, ysz, xsz = field.shape
    blocks = field.reshape(zsz // 2, 2, ysz // 2, 2, xsz // 2, 2)
    return jnp.sum(blocks, axis=(1, 3, 5)) * 0.125


def prolong(field):
    return jnp.repeat(jnp.repeat(jnp.repeat(field, 2, 0), 2, 1), 2, 2)


def reference(charge):
    source0 = four_pi * charge
    pre0 = smooth(jnp.zeros_like(source0), source0, 1.0, NU)
    source1 = restrict(source0 - operate(pre0, 1.0))
    pre1 = smooth(jnp.zeros_like(source1), source1, 0.25, NU)
    source2 = restrict(source1 - operate(pre1, 0.25))
    coarse = smooth(jnp.zeros_like(source2), source2, 0.0625, COARSE_SWEEPS)
    post1 = smooth(pre1 + prolong(coarse), source1, 0.25, NU)
    return smooth(pre0 + prolong(post1), source0, 1.0, NU)
```

```python
import functools

import jax
import jax.numpy as jnp
from jax import lax
from jax.experimental import pallas as pl
from jax.experimental.pallas import tpu as pltpu
from jax.sharding import PartitionSpec as P

COARSE_SWEEPS = 12
KAPPA = 0.001
OMEGA = 0.8
FOUR_PI = 12.566370614359172
MESH = pl.DeviceIdType.MESH
F32 = jnp.float32


class Level:
    def __init__(self, scale):
        self.c = OMEGA / (6.0 * scale + KAPPA)
        self.a = 1.0 - OMEGA
        self.b = self.c * scale
        self.r = self.a / self.b
        self.t = 2.0 * self.b * self.b
        self.rho = self.r + 2.0
        self.alpha = (self.a**2 + 6.0 * self.a * self.b + 12.0 * self.b**2) / self.t


L0, L1, L2 = Level(1.0), Level(0.25), Level(0.0625)
SIGMA1 = FOUR_PI * L0.t / 8.0
SIGMA2 = SIGMA1 * L1.t / 8.0


def lane_of(n):
    return lax.broadcasted_iota(jnp.int32, (n, 128), 1)


def take(v, idx):
    return jnp.take_along_axis(v, idx, axis=1, mode="promise_in_bounds")


def shift_tables(n):
    lane = lane_of(n)
    up = jnp.where(lane < 124, lane + 4, (lane + 1) % 4)
    down = jnp.where(lane < 4, 124 + (lane + 3) % 4, lane - 4)
    return up, down


def x_up(v, up):
    return v[1:] + [take(v[0], up)]


def x_down(v, down):
    return [take(v[-1], down)] + v[:-1]


def swap(p, q, bit, lane):
    clear = (lane & bit) == 0
    t = take(jnp.where(clear, q, p), lane ^ bit)
    return jnp.where(clear, p, t), jnp.where(clear, t, q)


def to_groups(v, lane):
    a0, a1 = swap(v[0], v[1], 1, lane)
    a2, a3 = swap(v[2], v[3], 1, lane)
    b0, b2 = swap(a0, a2, 2, lane)
    b1, b3 = swap(a1, a3, 2, lane)
    return [b0, b1, b2, b3]


def from_groups(v, lane):
    b0, b2 = swap(v[0], v[2], 2, lane)
    b1, b3 = swap(v[1], v[3], 2, lane)
    a0, a1 = swap(b0, b1, 1, lane)
    a2, a3 = swap(b2, b3, 1, lane)
    return [a0, a1, a2, a3]


def add(*lists):
    out = lists[0]
    for l in lists[1:]:
        out = [a + b for a, b in zip(out, l)]
    return out


def mul(k, v):
    return [k * a for a in v]


def restrict_parts(load, lv, up, down):
    E, V = {}, {}
    for pz in (0, 1):
        for py in (0, 1):
            lo, hi = load(pz, py)
            E[pz, py] = add(lo, hi)
            V[pz, py] = add(x_up(lo, up), x_down(hi, down))
    K = {k: add(mul(lv.rho, E[k]), V[k]) for k in E}
    p = add(E[0, 0], E[0, 1], E[1, 0], E[1, 1])
    hp = mul(0.5, p)
    n0 = add(mul(lv.alpha, p), x_up(hp, up), x_down(hp, down))
    n0 = add(n0, mul(lv.rho, add(V[0, 0], V[0, 1], V[1, 0], V[1, 1])))
    nu = add(hp, K[0, 0], K[1, 0])
    nd = add(hp, K[0, 1], K[1, 1])
    zu = add(hp, K[0, 0], K[0, 1])
    zd = add(hp, K[1, 0], K[1, 1])
    return [n0, nu, nd, zu, E[0, 0], E[0, 1], zd, E[1, 0], E[1, 1]]


def gather_parts(T, z, j, row, n):
    here, above, below = pl.ds(row, n), pl.ds(row + 1, n), pl.ds(row - 1, n)
    out = T[0, z, j, here, :] + T[3, z + 1, j, here, :] + T[6, z - 1, j, here, :]
    out = out + (T[1, z, j, above, :] + T[4, z + 1, j, above, :] + T[7, z - 1, j, above, :])
    return out + (T[2, z, j, below, :] + T[5, z + 1, j, below, :] + T[8, z - 1, j, below, :])


def prolong_parts(q, lv, up, down):
    c = q(0, 0)
    zs, ys = (q(-1, 0), q(1, 0)), (q(0, -1), q(0, 1))
    n = add(zs[0], zs[1], ys[0], ys[1], x_up(c, up), x_down(c, down))
    n = add(mul(lv.alpha, c), mul(0.5, n))
    rc = mul(lv.rho, c)
    out = {}
    for pz in (0, 1):
        for py in (0, 1):
            s = add(zs[pz], ys[py])
            w = add(rc, s)
            A = add(n, mul(lv.rho, s), q(2 * pz - 1, 2 * py - 1))
            lo, hi = add(A, x_down(w, down)), add(A, x_up(w, up))
            out[pz, py] = [v for pair in zip(lo, hi) for v in pair]
    return out


def source_kernel(x_ref, f_ref, s1_ref, s2_ref, T0, T1):
    step = pl.program_id(0)
    planes = x_ref.shape[0]
    lane = lane_of(8)
    up, down = shift_tables(8)

    @pl.when(step == 0)
    def _():
        def clear(i, _):
            for z in (0, 1, 10, 11):
                T0[i, z] = jnp.zeros((2, 64, 128), F32)
            for z in range(2, 10):
                T0[i, z, :, 0:16, :] = jnp.zeros((2, 16, 128), F32)
                T0[i, z, :, 48:64, :] = jnp.zeros((2, 16, 128), F32)
            T1[i] = jnp.zeros(T1.shape[1:], F32)
            return 0

        lax.fori_loop(0, 9, clear, 0)
        s1_ref[0] = jnp.zeros(s1_ref.shape[1:], F32)
        s1_ref[11] = jnp.zeros(s1_ref.shape[1:], F32)

    def reorder(z, _):
        for r in range(0, 64, 8):
            v = [x_ref[z, pl.ds(r, 8), pl.ds(128 * k, 128)] for k in range(4)]
            for j, w in enumerate(to_groups(v, lane)):
                f_ref[z, j, pl.ds(r, 8), :] = w
        return 0

    lax.fori_loop(0, planes, reorder, 0, unroll=2)

    def parts0(i, _):
        for y in range(0, 32, 8):

            def load(pz, py):
                rows = pl.ds(2 * y + py, 8, stride=2)
                v = [f_ref[2 * i + pz, j, rows, :] for j in range(4)]
                return v[0::2], v[1::2]

            for k, part in enumerate(restrict_parts(load, L0, up, down)):
                for j, v in enumerate(part):
                    T0[k, step * (planes // 2) + i + 2, j, pl.ds(16 + y, 8), :] = v
        return 0

    lax.fori_loop(0, planes // 2, parts0, 0, unroll=True)

    @pl.when(step == pl.num_programs(0) - 1)
    def _():
        def sums0(z, _):
            for j in (0, 1):
                for r in range(0, 48, 8):
                    s1_ref[z, j, pl.ds(r, 8), :] = gather_parts(T0, z, j, r + 8, 8)
            return 0

        lax.fori_loop(1, 11, sums0, 0, unroll=2)

        def parts1(i, _):
            for y in (-4, 4, 12):

                def load(pz, py):
                    rows = pl.ds(2 * y + py + 8, 8, stride=2)
                    v = [s1_ref[2 * i + pz, j, rows, :] for j in (0, 1)]
                    return v[0:1], v[1:2]

                for k, part in enumerate(restrict_parts(load, L1, up, down)):
                    T1[k, i + 2, 0, pl.ds(16 + y, 8), :] = part[0]
            return 0

        lax.fori_loop(0, 6, parts1, 0, unroll=True)

        def sums1(z, _):
            for r in range(0, 32, 8):
                s2_ref[z, pl.ds(r, 8), :] = gather_parts(T1, z + 1, 0, r + 8, 8)
            return 0

        lax.fori_loop(0, 8, sums1, 0, unroll=2)


def local_sources(charge):
    step = 4
    return pl.pallas_call(
        source_kernel,
        grid=(16 // step,),
        in_specs=[pl.BlockSpec((step, 64, 512), lambda i: (i, 0, 0))],
        out_specs=[
            pl.BlockSpec((step, 4, 64, 128), lambda i: (i, 0, 0, 0)),
            pl.BlockSpec((12, 2, 48, 128), lambda i: (0, 0, 0, 0)),
            pl.BlockSpec((8, 32, 128), lambda i: (0, 0, 0)),
        ],
        out_shape=[
            jax.ShapeDtypeStruct((16, 4, 64, 128), F32),
            jax.ShapeDtypeStruct((12, 2, 48, 128), F32),
            jax.ShapeDtypeStruct((8, 32, 128), F32),
        ],
        scratch_shapes=[pltpu.VMEM((9, 12, 2, 64, 128), F32), pltpu.VMEM((9, 10, 1, 48, 128), F32)],
        compiler_params=pltpu.CompilerParams(vmem_limit_bytes=40 << 20),
    )(charge)


def sweep(dst, src, f, planes, rows, J, lv, kf, kb, f_off, d_off, unroll=2, tables=None):
    first, count = planes
    up, down = tables

    def plane(z, _):
        for row in range(rows[0], rows[0] + rows[1], 8):
            here = pl.ds(row, 8)
            v = [src[z, j, here, :] for j in range(J)]
            left, right = x_down(v, down), x_up(v, up)
            for j in range(J):
                s = (left[j] + right[j]) + (src[z - 1, j, here, :] + src[z + 1, j, here, :])
                s = s + (src[z, j, pl.ds(row - 1, 8), :] + src[z, j, pl.ds(row + 1, 8), :])
                s = kb * (s + lv.r * v[j])
                g = f[z + f_off[0], j, pl.ds(row + f_off[1], 8), :]
                dst[z + d_off[0], j, pl.ds(row + d_off[1], 8), :] = s + (g if kf == 1.0 else kf * g)
        return 0

    lax.fori_loop(first, first + count, plane, 0, unroll=unroll)


NEAR = [(dz, dy) for dz in (-1, 0, 1) for dy in (-1, 0, 1) if (dz, dy) != (0, 0)]
FAR = [(k, dy) for k in range(-4, 5) for dy in (-1, 0, 1) if (k, dy) != (0, 0)]


def pick(d, neg, zero, pos):
    return (zero, pos, neg)[d]


def exchange_kernel(f_ref, s1_ref, s2_ref, b0_ref, q_ref, FX, H1, H2, HB, SX, G1, G2, B1, S2X, U0, U1,
                    Z2, Y2, C2, Z1, Y1, C1, local, sf, rf, s1s, s1r, e1s, e1r, e2s, e2r):
    slab, col = lax.axis_index("slab"), lax.axis_index("col")
    slabs, cols = lax.axis_size("slab"), lax.axis_size("col")
    tables = shift_tables(8)

    def target(o):
        return (lax.rem(slab + o[0] + slabs, slabs), lax.rem(col + o[1] + cols, cols))

    own = pltpu.make_async_copy(f_ref, FX.at[pl.ds(3, 16), :, pl.ds(8, 64), :], local.at[0])
    own.start()
    barrier = pltpu.get_barrier_semaphore()
    for o in FAR:
        pl.semaphore_signal(barrier, inc=1, device_id=target(o), device_id_type=MESH)
    pl.semaphore_wait(barrier, len(FAR))

    def send(src, dst, ss, rs, k, o):
        copy = pltpu.make_async_remote_copy(
            src_ref=src, dst_ref=dst, send_sem=ss.at[k], recv_sem=rs.at[k], device_id=target(o), device_id_type=MESH
        )
        copy.start()
        return copy

    def slot(Z, Y, C, o):
        dz, dy = o
        if dy == 0:
            return Z.at[(dz + 1) // 2]
        if dz == 0:
            return Y.at[(dy + 1) // 2]
        return C.at[(dz + 1) + (dy + 1) // 2]

    first = []
    for k, o in enumerate(NEAR):
        z = pick(o[0], pl.ds(0, 2), pl.ds(2, 4), pl.ds(6, 2))
        y = pick(o[1], pl.ds(0, 8), pl.ds(8, 16), pl.ds(24, 8))
        first.append(send(s2_ref.at[z, y], slot(Z2, Y2, C2, o), e1s, e1r, k, o))
    second = []
    for k, o in enumerate(NEAR):
        z = pick(o[0], pl.ds(1, 5), pl.ds(1, 10), pl.ds(6, 5))
        y = pick(o[1], pl.ds(7, 5), pl.ds(7, 34), pl.ds(36, 5))
        second.append(send(s1_ref.at[z, :, y], slot(Z1, Y1, C1, o), s1s, s1r, k, o))
    own.wait()
    third = []
    for k, o in enumerate(NEAR):
        z = pick(o[0], pl.ds(3, 3), pl.ds(3, 16), pl.ds(16, 3))
        zt = pick(o[0], pl.ds(19, 3), pl.ds(3, 16), pl.ds(0, 3))
        y = pick(o[1], pl.ds(8, 3), pl.ds(8, 64), pl.ds(69, 3))
        yt = pick(o[1], pl.ds(72, 3), pl.ds(8, 64), pl.ds(5, 3))
        third.append(send(FX.at[z, :, y], FX.at[zt, :, yt], sf, rf, k, o))

    mid = S2X.at[pl.ds(13, 4), 0, pl.ds(16, 16)]
    mid[...] = s2_ref[2:6, 8:24, :]
    for copy in first:
        copy.wait_recv()
    for k, o in enumerate(NEAR):
        z = pick(o[0], pl.ds(15, 2), pl.ds(13, 4), pl.ds(13, 2))
        y = pick(o[1], pl.ds(24, 8), pl.ds(16, 16), pl.ds(16, 8))
        S2X[z, 0, y, :] = S2X[z, 0, y, :] + slot(Z2, Y2, C2, o)[...]
    fourth = []
    for k, o in enumerate(FAR):
        d, dy = o
        p0, np_ = (3, 1) if d == 4 else (0, 1) if d == -4 else (0, 4)
        r0, nr = (0, 16) if dy == 0 or abs(d) < 3 else (8, 8) if dy == 1 else (0, 8)
        src = S2X.at[pl.ds(13 + p0, np_), 0, pl.ds(16 + r0, nr)]
        dst = S2X.at[pl.ds(13 + p0 - 4 * d, np_), 0, pl.ds(16 + r0 - 16 * dy, nr)]
        fourth.append(send(src, dst, e2s, e2r, k, o))

    SX[2:14] = s1_ref[...]
    for z in (0, 1, 14, 15):
        SX[z] = jnp.zeros(SX.shape[1:], F32)
    for copy in second:
        copy.wait_recv()
    for k, o in enumerate(NEAR):
        z = pick(o[0], pl.ds(11, 5), pl.ds(3, 10), pl.ds(0, 5))
        y = pick(o[1], pl.ds(39, 5), pl.ds(7, 34), pl.ds(4, 5))
        SX[z, :, y, :] = SX[z, :, y, :] + slot(Z1, Y1, C1, o)[...]
    run = functools.partial(sweep, J=2, lv=L1, tables=tables, f_off=(0, 0))
    run(G1, SX, SX, (1, 14), (5, 40), kf=1.0, kb=L1.b, d_off=(0, 0))
    run(G2, G1, SX, (2, 12), (6, 40), kf=1.0, kb=L1.b, d_off=(0, 0))
    k1 = L0.t * L1.c * SIGMA1
    run(B1, G2, SX, (3, 10), (7, 40), kf=k1, kb=k1 * L1.b, d_off=(-2, 0))

    for copy in third:
        copy.wait_recv()
    run = functools.partial(sweep, J=4, lv=L0, tables=tables, f_off=(0, 0))
    run(H1, FX, FX, (1, 20), (6, 72), kf=1.0, kb=L0.b, d_off=(0, 0))
    run(H2, H1, FX, (2, 18), (7, 72), kf=1.0, kb=L0.b, d_off=(0, 0))
    k0 = FOUR_PI * L0.c
    run(HB, H2, FX, (3, 16), (8, 64), kf=k0, kb=k0 * L0.b, d_off=(-3, -8))
    out = pltpu.make_async_copy(HB, b0_ref, local.at[1])
    out.start()

    for copy in fourth:
        copy.wait_recv()
    src = S2X
    k2 = L0.t * L1.t * L2.c * SIGMA2
    for n in range(1, COARSE_SWEEPS):
        dst = (U0, U1)[n % 2]
        last = n == COARSE_SWEEPS - 1
        rows = 16 + 2 * (13 - n)
        sweep(dst, src, S2X, (n, 30 - 2 * n), (3 + n, -(-rows // 8) * 8), 1, L2, k2 if last else 1.0,
              k2 * L2.b if last else L2.b, (0, 0), (0, 0), tables=tables)
        src = dst

    def children(i, _):
        for y in (-4, 4, 12):
            q = lambda dz, dy: [src[i + 12 + dz, 0, pl.ds(16 + y + dy, 8), :]]
            for (pz, py), kids in prolong_parts(q, L1, *tables).items():
                rows = pl.ds(2 * y + py + 8, 8, stride=2)
                for j, v in enumerate(kids):
                    q_ref[2 * i + pz, j, rows, :] = v + B1[2 * i + pz, j, rows, :]
        return 0

    lax.fori_loop(0, 6, children, 0, unroll=2)

    out.wait()
    for copy in first + second + third + fourth:
        copy.wait_send()


def exchange(f, s1, s2):
    any_, vmem = pl.BlockSpec(memory_space=pl.ANY), pl.BlockSpec(memory_space=pltpu.VMEM)
    big, mid, small = (22, 4, 80, 128), (16, 2, 48, 128), (30, 1, 48, 128)
    shapes = [big, big, big, (16, 4, 64, 128), mid, mid, mid, (12, 2, 48, 128), small, small, small,
              (2, 2, 16, 128), (2, 4, 8, 128), (4, 2, 8, 128), (2, 5, 2, 34, 128), (2, 10, 2, 5, 128), (4, 5, 2, 5, 128)]
    return pl.pallas_call(
        exchange_kernel,
        in_specs=[any_, vmem, vmem],
        out_specs=[any_, vmem],
        out_shape=[jax.ShapeDtypeStruct((16, 4, 64, 128), F32), jax.ShapeDtypeStruct((12, 2, 48, 128), F32)],
        scratch_shapes=[pltpu.VMEM(s, F32) for s in shapes]
        + [pltpu.SemaphoreType.DMA((2,))]
        + [pltpu.SemaphoreType.DMA((n,)) for n in (8, 8, 8, 8, 8, 8, len(FAR), len(FAR))],
        compiler_params=pltpu.CompilerParams(collective_id=0, has_side_effects=True, vmem_limit_bytes=48 << 20),
    )(f, s1, s2)


def fine_kernel(b_ref, q_ref, o_ref, W):
    step = pl.program_id(0)
    planes = b_ref.shape[0]
    tables = shift_tables(8)
    lane = lane_of(8)

    def pair(i, _):
        zc = step * (planes // 2) + i + 2
        for y in range(0, 32, 8):
            q = lambda dz, dy: [q_ref[zc + dz, j, pl.ds(8 + y + dy, 8), :] for j in (0, 1)]
            for (pz, py), kids in prolong_parts(q, L0, *tables).items():
                rows = pl.ds(2 * y + py, 8, stride=2)
                for j, v in enumerate(kids):
                    W[2 * i + pz, j, rows, :] = v + b_ref[2 * i + pz, j, rows, :]
        return 0

    lax.fori_loop(0, planes // 2, pair, 0, unroll=True)

    def reorder(z, _):
        for r in range(0, 64, 8):
            v = [W[z, j, pl.ds(r, 8), :] for j in range(4)]
            for k, w in enumerate(from_groups(v, lane)):
                o_ref[z, pl.ds(r, 8), pl.ds(128 * k, 128)] = w
        return 0

    lax.fori_loop(0, planes, reorder, 0, unroll=2)


def fine(b0, q):
    step = 4
    return pl.pallas_call(
        fine_kernel,
        grid=(16 // step,),
        in_specs=[
            pl.BlockSpec((step, 4, 64, 128), lambda i: (i, 0, 0, 0)),
            pl.BlockSpec((12, 2, 48, 128), lambda i: (0, 0, 0, 0)),
        ],
        out_specs=pl.BlockSpec((step, 64, 512), lambda i: (i, 0, 0)),
        out_shape=jax.ShapeDtypeStruct((16, 64, 512), F32),
        scratch_shapes=[pltpu.VMEM((step, 4, 64, 128), F32)],
        compiler_params=pltpu.CompilerParams(vmem_limit_bytes=24 << 20),
    )(b0, q)


def per_device(charge):
    f, s1, s2 = local_sources(charge)
    b0, q = exchange(f, s1, s2)
    return fine(b0, q)


def solution(mesh):
    placed = (P("slab", "col", None),)
    return jax.shard_map(
        per_device, mesh=mesh, in_specs=placed, out_specs=P("slab", "col", None), check_vma=False
    )
```

```python
import functools
import math

import jax
import jax.numpy as jnp
from jax import lax
from jax.experimental import pallas as pl
from jax.experimental.pallas import tpu as pltpu
from jax.sharding import PartitionSpec as P

COARSE_SWEEPS = 12
KAPPA = 0.001
OMEGA = 0.8
FOUR_PI = 12.566370614359172
MESH = pl.DeviceIdType.MESH
F32 = jnp.float32


class Level:
    def __init__(self, scale):
        self.c = OMEGA / (6.0 * scale + KAPPA)
        self.a = 1.0 - OMEGA
        self.b = self.c * scale
        self.r = self.a / self.b
        self.t = 2.0 * self.b * self.b
        self.rho = self.r + 2.0
        self.alpha = (self.a**2 + 6.0 * self.a * self.b + 12.0 * self.b**2) / self.t


L0, L1, L2 = Level(1.0), Level(0.25), Level(0.0625)
SIGMA1 = FOUR_PI * L0.t / 8.0
SIGMA2 = SIGMA1 * L1.t / 8.0


def lane_of(n):
    return lax.broadcasted_iota(jnp.int32, (n, 128), 1)


def take(v, idx):
    return jnp.take_along_axis(v, idx, axis=1, mode="promise_in_bounds")


def shift_tables(n):
    lane = lane_of(n)
    up = jnp.where(lane < 124, lane + 4, (lane + 1) % 4)
    down = jnp.where(lane < 4, 124 + (lane + 3) % 4, lane - 4)
    return up, down


def x_up(v, up):
    return v[1:] + [take(v[0], up)]


def x_down(v, down):
    return [take(v[-1], down)] + v[:-1]


def swap(p, q, bit, lane):
    clear = (lane & bit) == 0
    t = take(jnp.where(clear, q, p), lane ^ bit)
    return jnp.where(clear, p, t), jnp.where(clear, t, q)


def to_groups(v, lane):
    a0, a1 = swap(v[0], v[1], 1, lane)
    a2, a3 = swap(v[2], v[3], 1, lane)
    b0, b2 = swap(a0, a2, 2, lane)
    b1, b3 = swap(a1, a3, 2, lane)
    return [b0, b1, b2, b3]


def from_groups(v, lane):
    b0, b2 = swap(v[0], v[2], 2, lane)
    b1, b3 = swap(v[1], v[3], 2, lane)
    a0, a1 = swap(b0, b1, 1, lane)
    a2, a3 = swap(b2, b3, 1, lane)
    return [a0, a1, a2, a3]


def fourier_tables():
    lane, mode = lax.broadcasted_iota(jnp.int32, (128, 128), 0), lax.broadcasted_iota(jnp.int32, (128, 128), 1)
    cell = 32 * (lane % 4) + lane // 4
    freq = jnp.where(mode <= 64, mode, mode - 64)
    turn = (cell * freq + jnp.where(mode <= 64, 0, 96)) % 128
    single = (mode == 0) | (mode == 64)
    norm = jnp.where(single, math.sqrt(1.0 / 128.0), math.sqrt(2.0 / 128.0)).astype(F32)
    basis = norm * jnp.cos((2.0 * math.pi / 128.0) * turn.astype(F32))
    eigen = 2.0 * jnp.cos((2.0 * math.pi / 128.0) * freq[0:8].astype(F32)) + L2.r
    return basis, eigen


def transform(v, basis, dims):
    return lax.dot_general(v, basis, ((((1,), (dims,))), ((), ())), precision=lax.Precision.HIGHEST,
                           preferred_element_type=F32)


def add(*lists):
    out = lists[0]
    for l in lists[1:]:
        out = [a + b for a, b in zip(out, l)]
    return out


def mul(k, v):
    return [k * a for a in v]


def restrict_parts(load, lv, up, down):
    E, V = {}, {}
    for pz in (0, 1):
        for py in (0, 1):
            lo, hi = load(pz, py)
            E[pz, py] = add(lo, hi)
            V[pz, py] = add(x_up(lo, up), x_down(hi, down))
    K = {k: add(mul(lv.rho, E[k]), V[k]) for k in E}
    p = add(E[0, 0], E[0, 1], E[1, 0], E[1, 1])
    hp = mul(0.5, p)
    n0 = add(mul(lv.alpha, p), x_up(hp, up), x_down(hp, down))
    n0 = add(n0, mul(lv.rho, add(V[0, 0], V[0, 1], V[1, 0], V[1, 1])))
    nu = add(hp, K[0, 0], K[1, 0])
    nd = add(hp, K[0, 1], K[1, 1])
    zu = add(hp, K[0, 0], K[0, 1])
    zd = add(hp, K[1, 0], K[1, 1])
    return [n0, nu, nd, zu, E[0, 0], E[0, 1], zd, E[1, 0], E[1, 1]]


def gather_parts(T, z, j, row, n):
    here, above, below = pl.ds(row, n), pl.ds(row + 1, n), pl.ds(row - 1, n)
    out = T[0, z, j, here, :] + T[3, z + 1, j, here, :] + T[6, z - 1, j, here, :]
    out = out + (T[1, z, j, above, :] + T[4, z + 1, j, above, :] + T[7, z - 1, j, above, :])
    return out + (T[2, z, j, below, :] + T[5, z + 1, j, below, :] + T[8, z - 1, j, below, :])


def prolong_parts(q, lv, up, down):
    c = q(0, 0)
    zs, ys = (q(-1, 0), q(1, 0)), (q(0, -1), q(0, 1))
    n = add(zs[0], zs[1], ys[0], ys[1], x_up(c, up), x_down(c, down))
    n = add(mul(lv.alpha, c), mul(0.5, n))
    rc = mul(lv.rho, c)
    out = {}
    for pz in (0, 1):
        for py in (0, 1):
            s = add(zs[pz], ys[py])
            w = add(rc, s)
            A = add(n, mul(lv.rho, s), q(2 * pz - 1, 2 * py - 1))
            lo, hi = add(A, x_down(w, down)), add(A, x_up(w, up))
            out[pz, py] = [v for pair in zip(lo, hi) for v in pair]
    return out


CHUNK = 2


def chunk_at(i):
    return (i % 2) * (16 // CHUNK - 1 - i // 2) + (1 - i % 2) * (i // 2)


def local_sources(X, arrived, met, FX, s1_ref, s2_ref, T0, T1):
    lane = lane_of(8)
    up, down = shift_tables(8)

    def clear(i, _):
        for z in (0, 1, 10, 11):
            T0[i, z] = jnp.zeros((2, 64, 128), F32)
        for z in range(2, 10):
            T0[i, z, :, 0:16, :] = jnp.zeros((2, 16, 128), F32)
            T0[i, z, :, 48:64, :] = jnp.zeros((2, 16, 128), F32)
        T1[i] = jnp.zeros(T1.shape[1:], F32)
        return 0

    lax.fori_loop(0, 9, clear, 0)
    s1_ref[0] = jnp.zeros(s1_ref.shape[1:], F32)
    s1_ref[11] = jnp.zeros(s1_ref.shape[1:], F32)

    def chunk(i, _):
        c = chunk_at(i)
        arrived(c)
        for i in range(CHUNK):
            z = c * CHUNK + i
            for r in range(0, 64, 8):
                v = [X[z, pl.ds(r, 8), pl.ds(128 * k, 128)] for k in range(4)]
                for j, w in enumerate(to_groups(v, lane)):
                    FX[z + 3, j, pl.ds(8 + r, 8), :] = w
        for i in range(CHUNK // 2):
            zc = c * (CHUNK // 2) + i
            for y in range(0, 32, 8):

                def load(pz, py):
                    rows = pl.ds(8 + 2 * y + py, 8, stride=2)
                    v = [FX[2 * zc + pz + 3, j, rows, :] for j in range(4)]
                    return v[0::2], v[1::2]

                for k, part in enumerate(restrict_parts(load, L0, up, down)):
                    for j, v in enumerate(part):
                        T0[k, zc + 2, j, pl.ds(16 + y, 8), :] = v
        return 0

    lax.fori_loop(0, 4, chunk, 0)
    met()
    lax.fori_loop(4, 16 // CHUNK, chunk, 0)

    def sums0(z, _):
        for j in (0, 1):
            for r in range(0, 48, 8):
                s1_ref[z, j, pl.ds(r, 8), :] = gather_parts(T0, z, j, r + 8, 8)
        return 0

    lax.fori_loop(1, 11, sums0, 0, unroll=2)

    def parts1(i, _):
        for y in (-4, 4, 12):

            def load(pz, py):
                rows = pl.ds(2 * y + py + 8, 8, stride=2)
                v = [s1_ref[2 * i + pz, j, rows, :] for j in (0, 1)]
                return v[0:1], v[1:2]

            for k, part in enumerate(restrict_parts(load, L1, up, down)):
                T1[k, i + 2, 0, pl.ds(16 + y, 8), :] = part[0]
        return 0

    lax.fori_loop(0, 6, parts1, 0, unroll=True)

    def sums1(z, _):
        for r in range(0, 32, 8):
            s2_ref[z, pl.ds(r, 8), :] = gather_parts(T1, z + 1, 0, r + 8, 8)
        return 0

    lax.fori_loop(0, 8, sums1, 0, unroll=2)


def sweep(dst, src, f, planes, rows, J, lv, kf, kb, f_off, d_off, unroll=2, tables=None):
    first, count = planes
    up, down = tables

    def plane(z, _):
        for row in range(rows[0], rows[0] + rows[1], 8):
            here = pl.ds(row, 8)
            v = [src[z, j, here, :] for j in range(J)]
            left, right = x_down(v, down), x_up(v, up)
            for j in range(J):
                s = (left[j] + right[j]) + (src[z - 1, j, here, :] + src[z + 1, j, here, :])
                s = s + (src[z, j, pl.ds(row - 1, 8), :] + src[z, j, pl.ds(row + 1, 8), :])
                s = kb * (s + lv.r * v[j])
                g = f[z + f_off[0], j, pl.ds(row + f_off[1], 8), :]
                dst[z + d_off[0], j, pl.ds(row + d_off[1], 8), :] = s + (g if kf == 1.0 else kf * g)
        return 0

    lax.fori_loop(first, first + count, plane, 0, unroll=unroll)


def modal_sweep(dst, src, f, eigen, planes, rows, kf, kb):
    eig = eigen[...]

    def plane(z, _):
        for row in range(rows[0], rows[0] + rows[1], 8):
            here = pl.ds(row, 8)
            s = src[z - 1, 0, here, :] + src[z + 1, 0, here, :]
            s = s + (src[z, 0, pl.ds(row - 1, 8), :] + src[z, 0, pl.ds(row + 1, 8), :])
            g = f[z, 0, here, :]
            dst[z, 0, here, :] = kb * (s + eig * src[z, 0, here, :]) + (g if kf == 1.0 else kf * g)
        return 0

    lax.fori_loop(planes[0], planes[0] + planes[1], plane, 0, unroll=4)


NEAR = [(dz, dy) for dz in (-1, 0, 1) for dy in (-1, 0, 1) if (dz, dy) != (0, 0)]
FAR = [(k, dy) for k in range(-4, 5) for dy in (-1, 0, 1) if (k, dy) != (0, 0)]


def pick(d, neg, zero, pos):
    return (zero, pos, neg)[d]


def exchange_kernel(x_ref, b0_ref, q_ref, basis, eigen, X, T0, T1, s1_ref, s2_ref, FX, H1, H2, SX, G1, G2, B1, S2X, U0, U1,
                    Z2, Y2, C2, Z1, Y1, C1, load_sem, sf, rf, s1s, s1r, e1s, e1r, e2s, e2r):
    slab, col = lax.axis_index("slab"), lax.axis_index("col")
    slabs, cols = lax.axis_size("slab"), lax.axis_size("col")
    tables = shift_tables(8)

    def target(o):
        return (lax.rem(slab + o[0] + slabs, slabs), lax.rem(col + o[1] + cols, cols))

    def fetch(c):
        part = pl.ds(c * CHUNK, CHUNK)
        return pltpu.make_async_copy(x_ref.at[part], X.at[part], load_sem.at[c])

    for i in range(16 // CHUNK):
        fetch(chunk_at(i)).start()
    barrier = pltpu.get_barrier_semaphore()
    for o in FAR:
        pl.semaphore_signal(barrier, inc=1, device_id=target(o), device_id_type=MESH)
    def send(src, dst, ss, rs, k, o):
        copy = pltpu.make_async_remote_copy(
            src_ref=src, dst_ref=dst, send_sem=ss.at[k], recv_sem=rs.at[k], device_id=target(o), device_id_type=MESH
        )
        copy.start()
        return copy

    third = []

    full = (8, 8, 64)
    along_z = [((1, 0), (17, 1, 2), full), ((-1, 0), (3, 19, 2), full)]
    outer = [((1, 0), (16, 0, 1), full), ((-1, 0), (5, 21, 1), full)]
    rest = []
    for dy, rows in ((1, (69, 5, 3)), (-1, (8, 72, 3))):
        rest += [((0, dy), (3, 3, 16), rows), ((1, dy), (16, 0, 3), rows), ((-1, dy), (3, 19, 3), rows)]

    def fine_layers(pieces):
        for o, (z, zt, nz), (y, yt, ny) in pieces:
            src = FX.at[pl.ds(z, nz), :, pl.ds(y, ny)]
            third.append(send(src, FX.at[pl.ds(zt, nz), :, pl.ds(yt, ny)], sf, rf, len(third), o))

    def met():
        pl.semaphore_wait(barrier, len(FAR))
        fine_layers(along_z)

    local_sources(X, lambda c: fetch(c).wait(), met, FX, s1_ref, s2_ref, T0, T1)

    def slot(Z, Y, C, o):
        dz, dy = o
        if dy == 0:
            return Z.at[(dz + 1) // 2]
        if dz == 0:
            return Y.at[(dy + 1) // 2]
        return C.at[(dz + 1) + (dy + 1) // 2]

    first = []
    for k, o in enumerate(NEAR):
        z = pick(o[0], pl.ds(0, 2), pl.ds(2, 4), pl.ds(6, 2))
        y = pick(o[1], pl.ds(0, 8), pl.ds(8, 16), pl.ds(24, 8))
        first.append(send(s2_ref.at[z, y], slot(Z2, Y2, C2, o), e1s, e1r, k, o))
    second = []
    for k, o in enumerate(NEAR):
        z = pick(o[0], pl.ds(1, 5), pl.ds(1, 10), pl.ds(6, 5))
        y = pick(o[1], pl.ds(7, 5), pl.ds(7, 34), pl.ds(36, 5))
        second.append(send(s1_ref.at[z, :, y], slot(Z1, Y1, C1, o), s1s, s1r, k, o))
    fine_layers(rest)

    fine_layers(outer)
    mid = S2X.at[pl.ds(13, 4), 0, pl.ds(16, 16)]
    mid[...] = s2_ref[2:6, 8:24, :]
    basis[...], eigen[...] = fourier_tables()
    for copy in first:
        copy.wait_recv()
    for k, o in enumerate(NEAR):
        z = pick(o[0], pl.ds(15, 2), pl.ds(13, 4), pl.ds(13, 2))
        y = pick(o[1], pl.ds(24, 8), pl.ds(16, 16), pl.ds(16, 8))
        S2X[z, 0, y, :] = S2X[z, 0, y, :] + slot(Z2, Y2, C2, o)[...]
    S2X[13:17, 0, 16:32, :] = transform(mid[...].reshape(64, 128), basis[...], 0).reshape(4, 16, 128)
    fourth = []
    for k, o in enumerate(FAR):
        d, dy = o
        p0, np_ = (3, 1) if d == 4 else (0, 1) if d == -4 else (0, 4)
        nr = 16 if dy == 0 else (13, 13, 9, 5, 1)[abs(d)]
        r0 = 16 - nr if dy == 1 else 0
        src = S2X.at[pl.ds(13 + p0, np_), 0, pl.ds(16 + r0, nr)]
        dst = S2X.at[pl.ds(13 + p0 - 4 * d, np_), 0, pl.ds(16 + r0 - 16 * dy, nr)]
        fourth.append(send(src, dst, e2s, e2r, k, o))

    SX[2:14] = s1_ref[...]
    for z in (0, 1, 14, 15):
        SX[z] = jnp.zeros(SX.shape[1:], F32)
    for copy in second:
        copy.wait_recv()
    for k, o in enumerate(NEAR):
        z = pick(o[0], pl.ds(11, 5), pl.ds(3, 10), pl.ds(0, 5))
        y = pick(o[1], pl.ds(39, 5), pl.ds(7, 34), pl.ds(4, 5))
        SX[z, :, y, :] = SX[z, :, y, :] + slot(Z1, Y1, C1, o)[...]
    run = functools.partial(sweep, J=2, lv=L1, tables=tables, f_off=(0, 0))
    run(G1, SX, SX, (1, 14), (5, 40), kf=1.0, kb=L1.b, d_off=(0, 0))
    run(G2, G1, SX, (2, 12), (6, 40), kf=1.0, kb=L1.b, d_off=(0, 0))
    k1 = L0.t * L1.c * SIGMA1
    run(B1, G2, SX, (3, 10), (7, 40), kf=k1, kb=k1 * L1.b, d_off=(-2, 0))

    for copy in third:
        copy.wait_recv()
    run = functools.partial(sweep, J=4, lv=L0, tables=tables, f_off=(0, 0))
    run(H1, FX, FX, (1, 20), (6, 72), kf=1.0, kb=L0.b, d_off=(0, 0))
    run(H2, H1, FX, (2, 18), (7, 72), kf=1.0, kb=L0.b, d_off=(0, 0))
    k0 = FOUR_PI * L0.c
    run(b0_ref, H2, FX, (3, 16), (8, 64), kf=k0, kb=k0 * L0.b, d_off=(-3, -8))

    for copy in fourth:
        copy.wait_recv()
    src = S2X
    k2 = L0.t * L1.t * L2.c * SIGMA2
    for n in range(1, COARSE_SWEEPS):
        dst = (U0, U1)[n % 2]
        last = n == COARSE_SWEEPS - 1
        rows = 16 + 2 * (13 - n)
        kf, kb = (k2, k2 * L2.b) if last else (1.0, L2.b)
        modal_sweep(dst, src, S2X, eigen, (n, 30 - 2 * n), (3 + n, rows), kf, kb)
        src = dst
    U0[11:19, 0, 12:36, :] = transform(src[11:19, 0, 12:36, :].reshape(192, 128), basis[...], 1).reshape(8, 24, 128)
    src = U0

    def children(i, _):
        for y in (-4, 4, 12):
            q = lambda dz, dy: [src[i + 12 + dz, 0, pl.ds(16 + y + dy, 8), :]]
            for (pz, py), kids in prolong_parts(q, L1, *tables).items():
                rows = pl.ds(2 * y + py + 8, 8, stride=2)
                for j, v in enumerate(kids):
                    q_ref[2 * i + pz, j, rows, :] = v + B1[2 * i + pz, j, rows, :]
        return 0

    lax.fori_loop(0, 6, children, 0, unroll=2)

    for copy in first + second + third + fourth:
        copy.wait_send()


def exchange(charge):
    hbm, vmem = pl.BlockSpec(memory_space=pltpu.HBM), pl.BlockSpec(memory_space=pltpu.VMEM)
    big, mid, small = (22, 4, 80, 128), (16, 2, 48, 128), (30, 1, 48, 128)
    shapes = [(128, 128), (8, 128), (16, 64, 512), (9, 12, 2, 64, 128), (9, 10, 1, 48, 128), (12, 2, 48, 128), (8, 32, 128), big, big, big, mid, mid, mid, (12, 2, 48, 128), small, small, small,
              (2, 2, 16, 128), (2, 4, 8, 128), (4, 2, 8, 128), (2, 5, 2, 34, 128), (2, 10, 2, 5, 128), (4, 5, 2, 5, 128)]
    return pl.pallas_call(
        exchange_kernel,
        in_specs=[hbm],
        out_specs=[vmem, vmem],
        out_shape=[jax.ShapeDtypeStruct((16, 4, 64, 128), F32), jax.ShapeDtypeStruct((12, 2, 48, 128), F32)],
        scratch_shapes=[pltpu.VMEM(s, F32) for s in shapes]
        + [pltpu.SemaphoreType.DMA((16 // CHUNK,))]
        + [pltpu.SemaphoreType.DMA((n,)) for n in (10, 10, 8, 8, 8, 8, len(FAR), len(FAR))],
        compiler_params=pltpu.CompilerParams(collective_id=0, has_side_effects=True, vmem_limit_bytes=48 << 20),
    )(pltpu.with_memory_space_constraint(charge, pltpu.HBM))


def fine_kernel(b_ref, q_ref, o_ref, W, O, sems):
    tables = shift_tables(8)
    lane = lane_of(8)

    def store(i):
        part = pl.ds(i * CHUNK, CHUNK)
        return pltpu.make_async_copy(O.at[part], o_ref.at[part], sems.at[i])

    def pair(i, _):
        for y in range(0, 32, 8):
            q = lambda dz, dy: [q_ref[i + 2 + dz, j, pl.ds(8 + y + dy, 8), :] for j in (0, 1)]
            for (pz, py), kids in prolong_parts(q, L0, *tables).items():
                rows = pl.ds(2 * y + py, 8, stride=2)
                for j, v in enumerate(kids):
                    W[2 * i + pz, j, rows, :] = v + b_ref[2 * i + pz, j, rows, :]
        for z in range(2):
            for r in range(0, 64, 8):
                v = [W[2 * i + z, j, pl.ds(r, 8), :] for j in range(4)]
                for k, w in enumerate(from_groups(v, lane)):
                    O[2 * i + z, pl.ds(r, 8), pl.ds(128 * k, 128)] = w
        store(i).start()
        return 0

    lax.fori_loop(0, 8, pair, 0)
    for i in range(8):
        store(i).wait()


def fine(b0, q):
    vmem = pl.BlockSpec(memory_space=pltpu.VMEM)
    return pl.pallas_call(
        fine_kernel,
        in_specs=[vmem, vmem],
        out_specs=pl.BlockSpec(memory_space=pl.ANY),
        out_shape=jax.ShapeDtypeStruct((16, 64, 512), F32),
        scratch_shapes=[
            pltpu.VMEM((16, 4, 64, 128), F32),
            pltpu.VMEM((16, 64, 512), F32),
            pltpu.SemaphoreType.DMA((8,)),
        ],
        compiler_params=pltpu.CompilerParams(vmem_limit_bytes=24 << 20),
    )(b0, q)


def per_device(charge):
    b0, q = exchange(charge)
    return fine(b0, q)


def solution(mesh):
    placed = (P("slab", "col", None),)
    return jax.shard_map(
        per_device, mesh=mesh, in_specs=placed, out_specs=P("slab", "col", None), check_vma=False
    )
```

```python
import functools
import math

import jax
import jax.numpy as jnp
from jax import lax
from jax.experimental import pallas as pl
from jax.experimental.pallas import tpu as pltpu
from jax.sharding import PartitionSpec as P

COARSE_SWEEPS = 12
KAPPA = 0.001
OMEGA = 0.8
FOUR_PI = 12.566370614359172
MESH = pl.DeviceIdType.MESH
F32 = jnp.float32


class Level:
    def __init__(self, scale):
        self.c = OMEGA / (6.0 * scale + KAPPA)
        self.a = 1.0 - OMEGA
        self.b = self.c * scale
        self.r = self.a / self.b
        self.t = 2.0 * self.b * self.b
        self.rho = self.r + 2.0
        self.alpha = (self.a**2 + 6.0 * self.a * self.b + 12.0 * self.b**2) / self.t


L0, L1, L2 = Level(1.0), Level(0.25), Level(0.0625)
SIGMA1 = FOUR_PI * L0.t / 8.0
SIGMA2 = SIGMA1 * L1.t / 8.0


def lane_of(n):
    return lax.broadcasted_iota(jnp.int32, (n, 128), 1)


def take(v, idx):
    return jnp.take_along_axis(v, idx, axis=1, mode="promise_in_bounds")


def shift_tables(n):
    lane = lane_of(n)
    up = jnp.where(lane < 124, lane + 4, (lane + 1) % 4)
    down = jnp.where(lane < 4, 124 + (lane + 3) % 4, lane - 4)
    return up, down


def x_up(v, up):
    return v[1:] + [take(v[0], up)]


def x_down(v, down):
    return [take(v[-1], down)] + v[:-1]


def turn(v, lane):
    odd, high = (lane & 1) != 0, (lane & 2) != 0
    a = [jnp.where(odd, v[(d + 1) % 4], v[d]) for d in range(4)]
    return [jnp.where(high, a[(d + 2) % 4], a[d]) for d in range(4)]


def regroup(v, lane):
    v = turn(v, lane)
    v = v[:1] + [take(v[d], (lane & 124) | ((lane - d) & 3)) for d in (1, 2, 3)]
    v = turn(v, lane)
    return [v[0], v[3], v[2], v[1]]


def fourier_tables():
    lane, mode = lax.broadcasted_iota(jnp.int32, (128, 128), 0), lax.broadcasted_iota(jnp.int32, (128, 128), 1)
    cell = 32 * (lane % 4) + lane // 4
    freq = jnp.where(mode <= 64, mode, mode - 64)
    turn = (cell * freq + jnp.where(mode <= 64, 0, 96)) % 128
    single = (mode == 0) | (mode == 64)
    norm = jnp.where(single, math.sqrt(1.0 / 128.0), math.sqrt(2.0 / 128.0)).astype(F32)
    basis = norm * jnp.cos((2.0 * math.pi / 128.0) * turn.astype(F32))
    eigen = 2.0 * jnp.cos((2.0 * math.pi / 128.0) * freq[0:8].astype(F32)) + L2.r
    return basis, eigen


def transform(v, basis, dims):
    return lax.dot_general(v, basis, ((((1,), (dims,))), ((), ())), precision=lax.Precision.HIGHEST,
                           preferred_element_type=F32)


def add(*lists):
    out = lists[0]
    for l in lists[1:]:
        out = [a + b for a, b in zip(out, l)]
    return out


def mul(k, v):
    return [k * a for a in v]


def restrict_parts(load, lv, up, down):
    E, lo, hi = {}, {}, {}
    for k in ((0, 0), (0, 1), (1, 0), (1, 1)):
        lo[k], hi[k] = load(*k)
        E[k] = add(lo[k], hi[k])

    def pair(k, m):
        return add(mul(lv.rho, add(E[k], E[m])), x_up(add(lo[k], lo[m]), up), x_down(add(hi[k], hi[m]), down))

    z0, z1, y0 = pair((0, 0), (0, 1)), pair((1, 0), (1, 1)), pair((0, 0), (1, 0))
    total = add(z0, z1)
    y1 = [a - b for a, b in zip(total, y0)]
    p = add(E[0, 0], E[0, 1], E[1, 0], E[1, 1])
    hp = mul(0.5, p)
    n0 = add(mul(lv.alpha - lv.rho * lv.rho, p), x_up(hp, up), x_down(hp, down), mul(lv.rho, total))
    return [n0, add(hp, y0), add(hp, y1), add(hp, z0), E[0, 0], E[0, 1], add(hp, z1), E[1, 0], E[1, 1]]


def gather_parts(T, z, j, row, n):
    here, above, below = pl.ds(row, n), pl.ds(row + 1, n), pl.ds(row - 1, n)
    out = T[0, z, j, here, :] + T[3, z + 1, j, here, :] + T[6, z - 1, j, here, :]
    out = out + (T[1, z, j, above, :] + T[4, z + 1, j, above, :] + T[7, z - 1, j, above, :])
    return out + (T[2, z, j, below, :] + T[5, z + 1, j, below, :] + T[8, z - 1, j, below, :])


def prolong_parts(q, lv, up, down):
    c = q(0, 0)
    zs, ys = (q(-1, 0), q(1, 0)), (q(0, -1), q(0, 1))
    n = add(zs[0], zs[1], ys[0], ys[1], x_up(c, up), x_down(c, down))
    n = add(mul(lv.alpha, c), mul(0.5, n))
    rc = mul(lv.rho, c)
    w = {k: add(rc, zs[k[0]], ys[k[1]]) for k in ((0, 0), (0, 1), (1, 0))}
    lo = {k: x_down(v, down) for k, v in w.items()}
    hi = {k: x_up(v, up) for k, v in w.items()}
    for d in (lo, hi):
        d[1, 1] = [a + b - c for a, b, c in zip(d[0, 1], d[1, 0], d[0, 0])]
    out = {}
    for pz in (0, 1):
        for py in (0, 1):
            A = add(n, mul(lv.rho, add(zs[pz], ys[py])), q(2 * pz - 1, 2 * py - 1))
            out[pz, py] = [v for pair in zip(add(A, lo[pz, py]), add(A, hi[pz, py])) for v in pair]
    return out


CHUNK = 2


def chunk_at(i):
    return (i % 2) * (16 // CHUNK - 1 - i // 2) + (1 - i % 2) * (i // 2)


def local_sources(X, arrived, met, FX, s1_ref, s2_ref, T0, T1):
    lane = lane_of(8)
    up, down = shift_tables(8)

    def clear(i, _):
        for z in (0, 1, 10, 11):
            T0[i, z] = jnp.zeros((2, 64, 128), F32)
        for z in range(2, 10):
            T0[i, z, :, 0:16, :] = jnp.zeros((2, 16, 128), F32)
            T0[i, z, :, 48:64, :] = jnp.zeros((2, 16, 128), F32)
        T1[i] = jnp.zeros(T1.shape[1:], F32)
        return 0

    lax.fori_loop(0, 9, clear, 0)
    s1_ref[0] = jnp.zeros(s1_ref.shape[1:], F32)
    s1_ref[11] = jnp.zeros(s1_ref.shape[1:], F32)

    def chunk(i, _):
        c = chunk_at(i)
        arrived(c)
        for i in range(CHUNK):
            z = c * CHUNK + i
            for r in range(0, 64, 8):
                v = [X[z, pl.ds(r, 8), pl.ds(128 * k, 128)] for k in range(4)]
                for j, w in enumerate(regroup(v, lane)):
                    FX[z + 3, j, pl.ds(8 + r, 8), :] = w
        for i in range(CHUNK // 2):
            zc = c * (CHUNK // 2) + i
            for y in range(0, 32, 8):

                def load(pz, py):
                    rows = pl.ds(8 + 2 * y + py, 8, stride=2)
                    v = [FX[2 * zc + pz + 3, j, rows, :] for j in range(4)]
                    return v[0::2], v[1::2]

                for k, part in enumerate(restrict_parts(load, L0, up, down)):
                    for j, v in enumerate(part):
                        T0[k, zc + 2, j, pl.ds(16 + y, 8), :] = v
        return 0

    lax.fori_loop(0, 2, chunk, 0)
    met()
    lax.fori_loop(2, 16 // CHUNK, chunk, 0)

    def sums0(z, _):
        for j in (0, 1):
            for r in range(0, 48, 8):
                s1_ref[z, j, pl.ds(r, 8), :] = gather_parts(T0, z, j, r + 8, 8)
        return 0

    lax.fori_loop(1, 11, sums0, 0, unroll=2)

    def parts1(i, _):
        for y in (-4, 4, 12):

            def load(pz, py):
                rows = pl.ds(2 * y + py + 8, 8, stride=2)
                v = [s1_ref[2 * i + pz, j, rows, :] for j in (0, 1)]
                return v[0:1], v[1:2]

            for k, part in enumerate(restrict_parts(load, L1, up, down)):
                T1[k, i + 2, 0, pl.ds(16 + y, 8), :] = part[0]
        return 0

    lax.fori_loop(0, 6, parts1, 0, unroll=True)

    def sums1(z, _):
        for r in range(0, 32, 8):
            s2_ref[z, pl.ds(r, 8), :] = gather_parts(T1, z + 1, 0, r + 8, 8)
        return 0

    lax.fori_loop(0, 8, sums1, 0, unroll=2)


def sweep(dst, src, f, planes, rows, J, lv, kf, kb, f_off, d_off, unroll=2, tables=None):
    first, count = planes
    up, down = tables

    def plane(z, _):
        for row in range(rows[0], rows[0] + rows[1], 8):
            here = pl.ds(row, 8)
            v = [src[z, j, here, :] for j in range(J)]
            left, right = x_down(v, down), x_up(v, up)
            for j in range(J):
                s = (left[j] + right[j]) + (src[z - 1, j, here, :] + src[z + 1, j, here, :])
                s = s + (src[z, j, pl.ds(row - 1, 8), :] + src[z, j, pl.ds(row + 1, 8), :])
                s = kb * (s + lv.r * v[j])
                g = f[z + f_off[0], j, pl.ds(row + f_off[1], 8), :]
                dst[z + d_off[0], j, pl.ds(row + d_off[1], 8), :] = s + (g if kf == 1.0 else kf * g)
        return 0

    lax.fori_loop(first, first + count, plane, 0, unroll=unroll)


def modal_sweep(dst, src, f, eigen, planes, rows, kf, kb):
    eig = eigen[...]

    def plane(z, _):
        for row in range(rows[0], rows[0] + rows[1], 8):
            here = pl.ds(row, 8)
            s = src[z - 1, 0, here, :] + src[z + 1, 0, here, :]
            s = s + (src[z, 0, pl.ds(row - 1, 8), :] + src[z, 0, pl.ds(row + 1, 8), :])
            g = f[z, 0, here, :]
            dst[z, 0, here, :] = kb * (s + eig * src[z, 0, here, :]) + (g if kf == 1.0 else kf * g)
        return 0

    lax.fori_loop(planes[0], planes[0] + planes[1], plane, 0, unroll=4)


NEAR = [(dz, dy) for dz in (-1, 0, 1) for dy in (-1, 0, 1) if (dz, dy) != (0, 0)]
FAR = [(s * k, dy) for k in (4, 3, 2, 1, 0) for dy in (-1, 1, 0) for s in (1, -1) if (k, dy) != (0, 0) and (k or s == 1)]


def pick(d, neg, zero, pos):
    return (zero, pos, neg)[d]


def exchange_kernel(x_ref, b0_ref, q_ref, basis, eigen, X, T0, T1, s1_ref, s2_ref, FX, H1, H2, SX, G1, G2, B1, S2X, U0, U1,
                    Z2, Y2, C2, Z1, Y1, C1, load_sem, here, sf, rf, s1s, s1r, e1s, e1r, e2s, e2r):
    slab, col = lax.axis_index("slab"), lax.axis_index("col")
    slabs, cols = lax.axis_size("slab"), lax.axis_size("col")
    tables = shift_tables(8)

    def target(o):
        return (lax.rem(slab + o[0] + slabs, slabs), lax.rem(col + o[1] + cols, cols))

    def fetch(c):
        part = pl.ds(c * CHUNK, CHUNK)
        return pltpu.make_async_copy(x_ref.at[part], X.at[part], load_sem.at[c])

    for i in range(16 // CHUNK):
        fetch(chunk_at(i)).start()
    barrier = pltpu.get_barrier_semaphore()
    for o in NEAR:
        pl.semaphore_signal(barrier, inc=1, device_id=target(o), device_id_type=MESH)
    def send(src, dst, ss, rs, k, o):
        copy = pltpu.make_async_remote_copy(
            src_ref=src, dst_ref=dst, send_sem=ss.at[k], recv_sem=rs.at[k], device_id=target(o), device_id_type=MESH
        )
        copy.start()
        return copy

    third = []

    full = (8, 8, 64)
    along_z = [((1, 0), (17, 1, 2), full), ((-1, 0), (3, 19, 2), full)]
    outer = [((1, 0), (16, 0, 1), full), ((-1, 0), (5, 21, 1), full)]
    across, middle = [], []
    for dy, rows in ((1, (69, 5, 3)), (-1, (8, 72, 3))):
        across += [((1, dy), (16, 0, 3), rows), ((-1, dy), (3, 19, 3), rows)]
        across += [((0, dy), (3, 3, 4), rows), ((0, dy), (15, 15, 4), rows)]
        middle += [((0, dy), (7, 7, 8), rows)]

    def fine_layers(pieces):
        for o, (z, zt, nz), (y, yt, ny) in pieces:
            src = FX.at[pl.ds(z, nz), :, pl.ds(y, ny)]
            third.append(send(src, FX.at[pl.ds(zt, nz), :, pl.ds(yt, ny)], sf, rf, len(third), o))

    def tell(k):
        for o in ((k + 1, 0), (-k - 1, 0)):
            pl.semaphore_signal(here.at[k], inc=1, device_id=target(o), device_id_type=MESH)

    def heard(k):
        pl.semaphore_wait(here.at[k], 2)

    def met():
        pl.semaphore_wait(barrier, len(NEAR))
        fine_layers(along_z)
        tell(0)

    local_sources(X, lambda c: fetch(c).wait(), met, FX, s1_ref, s2_ref, T0, T1)

    def slot(Z, Y, C, o):
        dz, dy = o
        if dy == 0:
            return Z.at[(dz + 1) // 2]
        if dz == 0:
            return Y.at[(dy + 1) // 2]
        return C.at[(dz + 1) + (dy + 1) // 2]

    first = []
    for k, o in enumerate(NEAR):
        z = pick(o[0], pl.ds(0, 2), pl.ds(2, 4), pl.ds(6, 2))
        y = pick(o[1], pl.ds(6, 2), pl.ds(8, 16), pl.ds(24, 2))
        first.append(send(s2_ref.at[z, y], slot(Z2, Y2, C2, o), e1s, e1r, k, o))
    second = []
    for k, o in enumerate(NEAR):
        z = pick(o[0], pl.ds(1, 5), pl.ds(1, 10), pl.ds(6, 5))
        y = pick(o[1], pl.ds(7, 5), pl.ds(7, 34), pl.ds(36, 5))
        second.append(send(s1_ref.at[z, :, y], slot(Z1, Y1, C1, o), s1s, s1r, k, o))
    fine_layers(middle + across)

    fine_layers(outer)
    mid = S2X.at[pl.ds(13, 4), 0, pl.ds(16, 16)]
    mid[...] = s2_ref[2:6, 8:24, :]
    heard(0)
    tell(1)
    basis[...], eigen[...] = fourier_tables()
    for copy in first:
        copy.wait_recv()
    for k, o in enumerate(NEAR):
        z = pick(o[0], pl.ds(15, 2), pl.ds(13, 4), pl.ds(13, 2))
        y = pick(o[1], pl.ds(30, 2), pl.ds(16, 16), pl.ds(16, 2))
        S2X[z, 0, y, :] = S2X[z, 0, y, :] + slot(Z2, Y2, C2, o)[...]
    S2X[13:17, 0, 16:32, :] = transform(mid[...].reshape(64, 128), basis[...], 0).reshape(4, 16, 128)
    heard(1)
    fourth = []
    for k, o in enumerate(FAR):
        d, dy = o
        p0, np_ = (3, 1) if d == 4 else (0, 1) if d == -4 else (0, 4)
        nr = 16 if dy == 0 else (13, 13, 9, 5, 1)[abs(d)]
        r0 = 16 - nr if dy == 1 else 0
        src = S2X.at[pl.ds(13 + p0, np_), 0, pl.ds(16 + r0, nr)]
        dst = S2X.at[pl.ds(13 + p0 - 4 * d, np_), 0, pl.ds(16 + r0 - 16 * dy, nr)]
        fourth.append(send(src, dst, e2s, e2r, k, o))

    SX[2:14] = s1_ref[...]
    for z in (0, 1, 14, 15):
        SX[z] = jnp.zeros(SX.shape[1:], F32)
    for copy in second:
        copy.wait_recv()
    for k, o in enumerate(NEAR):
        z = pick(o[0], pl.ds(11, 5), pl.ds(3, 10), pl.ds(0, 5))
        y = pick(o[1], pl.ds(39, 5), pl.ds(7, 34), pl.ds(4, 5))
        SX[z, :, y, :] = SX[z, :, y, :] + slot(Z1, Y1, C1, o)[...]
    run = functools.partial(sweep, J=2, lv=L1, tables=tables, f_off=(0, 0))
    run(G1, SX, SX, (1, 14), (5, 40), kf=1.0, kb=L1.b, d_off=(0, 0))
    run(G2, G1, SX, (2, 12), (6, 40), kf=1.0, kb=L1.b, d_off=(0, 0))
    k1 = L0.t * L1.c * SIGMA1
    run(B1, G2, SX, (3, 10), (7, 40), kf=k1, kb=k1 * L1.b, d_off=(-2, 0))

    for copy in third:
        copy.wait_recv()
    run = functools.partial(sweep, J=4, lv=L0, tables=tables, f_off=(0, 0))
    run(H1, FX, FX, (1, 20), (6, 72), kf=1.0, kb=L0.b, d_off=(0, 0))
    run(H2, H1, FX, (2, 18), (7, 72), kf=1.0, kb=L0.b, d_off=(0, 0))
    k0 = FOUR_PI * L0.c
    run(b0_ref, H2, FX, (3, 16), (8, 64), kf=k0, kb=k0 * L0.b, d_off=(-3, -8))

    for copy in fourth:
        copy.wait_recv()
    src = S2X
    k2 = L0.t * L1.t * L2.c * SIGMA2
    for n in range(1, COARSE_SWEEPS):
        dst = (U0, U1)[n % 2]
        last = n == COARSE_SWEEPS - 1
        rows = 16 + 2 * (13 - n)
        kf, kb = (k2, k2 * L2.b) if last else (1.0, L2.b)
        modal_sweep(dst, src, S2X, eigen, (n, 30 - 2 * n), (3 + n, rows), kf, kb)
        src = dst
    U0[11:19, 0, 12:36, :] = transform(src[11:19, 0, 12:36, :].reshape(192, 128), basis[...], 1).reshape(8, 24, 128)
    src = U0

    def children(i, _):
        for y in (-4, 4, 12):
            q = lambda dz, dy: [src[i + 12 + dz, 0, pl.ds(16 + y + dy, 8), :]]
            for (pz, py), kids in prolong_parts(q, L1, *tables).items():
                rows = pl.ds(2 * y + py + 8, 8, stride=2)
                for j, v in enumerate(kids):
                    q_ref[2 * i + pz, j, rows, :] = v + B1[2 * i + pz, j, rows, :]
        return 0

    lax.fori_loop(0, 6, children, 0, unroll=2)

    for copy in first + second + third + fourth:
        copy.wait_send()


def exchange(charge):
    hbm, vmem = pl.BlockSpec(memory_space=pltpu.HBM), pl.BlockSpec(memory_space=pltpu.VMEM)
    big, mid, small = (22, 4, 80, 128), (16, 2, 48, 128), (30, 1, 48, 128)
    shapes = [(128, 128), (8, 128), (16, 64, 512), (9, 12, 2, 64, 128), (9, 10, 1, 48, 128), (12, 2, 48, 128), (8, 32, 128), big, big, big, mid, mid, mid, (12, 2, 48, 128), small, small, small,
              (2, 2, 16, 128), (2, 4, 2, 128), (4, 2, 2, 128), (2, 5, 2, 34, 128), (2, 10, 2, 5, 128), (4, 5, 2, 5, 128)]
    return pl.pallas_call(
        exchange_kernel,
        in_specs=[hbm],
        out_specs=[vmem, vmem],
        out_shape=[jax.ShapeDtypeStruct((16, 4, 64, 128), F32), jax.ShapeDtypeStruct((12, 2, 48, 128), F32)],
        scratch_shapes=[pltpu.VMEM(s, F32) for s in shapes]
        + [pltpu.SemaphoreType.DMA((16 // CHUNK,)), pltpu.SemaphoreType.REGULAR((2,))]
        + [pltpu.SemaphoreType.DMA((n,)) for n in (14, 14, 8, 8, 8, 8, len(FAR), len(FAR))],
        compiler_params=pltpu.CompilerParams(collective_id=0, has_side_effects=True, vmem_limit_bytes=48 << 20),
    )(pltpu.with_memory_space_constraint(charge, pltpu.HBM))


def fine_kernel(b_ref, q_ref, o_ref, W, O, sems):
    tables = shift_tables(8)
    lane = lane_of(8)

    def store(i):
        part = pl.ds(i * CHUNK, CHUNK)
        return pltpu.make_async_copy(O.at[part], o_ref.at[part], sems.at[i])

    def pair(i, _):
        for y in range(0, 32, 8):
            q = lambda dz, dy: [q_ref[i + 2 + dz, j, pl.ds(8 + y + dy, 8), :] for j in (0, 1)]
            for (pz, py), kids in prolong_parts(q, L0, *tables).items():
                rows = pl.ds(2 * y + py, 8, stride=2)
                for j, v in enumerate(kids):
                    W[2 * i + pz, j, rows, :] = v + b_ref[2 * i + pz, j, rows, :]
        for z in range(2):
            for r in range(0, 64, 8):
                v = [W[2 * i + z, j, pl.ds(r, 8), :] for j in range(4)]
                for k, w in enumerate(regroup(v, lane)):
                    O[2 * i + z, pl.ds(r, 8), pl.ds(128 * k, 128)] = w
        store(i).start()
        return 0

    lax.fori_loop(0, 8, pair, 0)
    for i in range(8):
        store(i).wait()


def fine(b0, q):
    vmem = pl.BlockSpec(memory_space=pltpu.VMEM)
    return pl.pallas_call(
        fine_kernel,
        in_specs=[vmem, vmem],
        out_specs=pl.BlockSpec(memory_space=pl.ANY),
        out_shape=jax.ShapeDtypeStruct((16, 64, 512), F32),
        scratch_shapes=[
            pltpu.VMEM((16, 4, 64, 128), F32),
            pltpu.VMEM((16, 64, 512), F32),
            pltpu.SemaphoreType.DMA((8,)),
        ],
        compiler_params=pltpu.CompilerParams(vmem_limit_bytes=24 << 20),
    )(b0, q)


def per_device(charge):
    b0, q = exchange(charge)
    return fine(b0, q)


def solution(mesh):
    placed = (P("slab", "col", None),)
    return jax.shard_map(
        per_device, mesh=mesh, in_specs=placed, out_specs=P("slab", "col", None), check_vma=False
    )
```
